32 devices in a mesh: px: 4 (over z), py: 8 (over y, x, core).
Axes of the slice: x: 2, y: 2, z: 4, core: 2. Of those that a mesh axis runs over, the one named last changes fastest.
Arguments:
- positions: float32 [8192, 3, 128], P(('px', 'py')), may hold values from 1 to 254, as said below
- strength: float32 [8192, 128], P(('px', 'py')), may hold values from -6 to 6
- destination: int32 [8192, 1], P(('px', 'py')), may hold values from 0 to 31; in each aligned block of 256 rows (0 to 255, 256 to 511, ...) at most 16 rows name the same one
- tile_index: int32 [8192], P(('px', 'py')), may hold values from 0 to 63
- particle_count: int32 [8192], P(('px', 'py')), may hold values from 1 to 128, 786432 in all
Outputs:
- spectrum: float32 [2, 512, 512, 256], P(None, 'px', 'py')
The draws below stay inside these ranges and needn't reach their ends.
Inputs may be any that keep to these rules, and one draw needn't show every extreme that they name: `destination`: among the 256 rows of one device no pencil is named more than 16 times; pencil index is i_px * 8 + i_py. `positions`: component 0 lies in [1, 14], component 1 in [1, 6], component 2 in [1, 254].
All inputs are finite; a program needn't handle non-finite values. No bound on the sum of `particle_count` on one device may be relied on, other than what follows from the above.
Results may differ from the reference program's by a relative error of at most 0.0003.
Values sent between devices are 32-bit elements; how exact they have to be, the bound alone decides.
No kernel may reach another device: no remote copies, remote signals or barrier semaphores. Data moves between devices by JAX's collectives and lax.ppermute only.
A program may use at most 192 MiB of HBM per device.

```python
import math
import jax
import jax.numpy as jnp
import numpy as np
from jax import lax

NX = 512
NY = 512
NZ = 256
BX = 16
BY = 8
PROW = 128
ROWS_DEV = 256
ROWS = 8192
CAP = 16
TILES = 64
N_PX = 4
N_PY = 8
DEVICES = 32


def draw_positions(key, part):
    unit = jax.random.uniform(key, (ROWS, 3, PROW), jnp.float32)
    upper_end = jnp.array([BX - 2.0, BY - 2.0, NZ - 2.0], jnp.float32)[None, :, None]
    return 1.0 + (upper_end - 1.0) * unit


def plant(values, rng, low, high):
    shape = values.shape
    place = [jax.random.randint(jax.random.fold_in(rng, axis), (), 0, shape[axis]) for axis in range(len(shape))]
    values = values.at[tuple(place)].set(low)
    longest = shape.index(max(shape))
    place[longest] = (place[longest] + 1) % shape[longest]
    return values.at[tuple(place)].set(high)


def level_of(key, dims, cuts, low, high):
    loudness = 1.0
    for dim, blocks in cuts:
        heights = jax.random.uniform(jax.random.fold_in(jax.random.fold_in(key, 6), dim), (blocks,), jnp.float32, low / len(cuts), high / len(cuts))
        loudness = loudness * jnp.repeat(jnp.exp(heights), dims[dim] // blocks).reshape((-1,) + (1,) * (len(dims) - 1 - dim))
    return loudness


def split_up(number_of, total, most, skew):
    loads = [(1 << 20) // math.isqrt(grade ** skew) + 1 for grade in range(2, number_of + 1)]
    spare, holding = total - most - (number_of - 1), [1] * (number_of - 1)
    while spare > 0:
        movable = [i for i in range(number_of - 1) if holding[i] < most]
        whole, left = sum([loads[i] for i in movable]), spare
        for i in movable:
            more = min(most - holding[i], max(1, left * loads[i] // whole), spare)
            holding[i] = holding[i] + more
            spare = spare - more
    return np.array([most] + holding)


def ragged(rng, amount, total, reach, skew):
    if amount == 2:
        one = jax.random.randint(rng, (), max(1, total - reach), min(reach, total - 1) + 1)
        return jnp.stack([one, total - one])
    lengths = jnp.asarray(split_up(amount, total, reach, skew), jnp.int32)
    pairs = (amount - 1) // 2
    giver, receiver = lengths[1:1 + 2 * pairs:2], lengths[2:2 + 2 * pairs:2]
    slack = jnp.minimum(giver - 1, reach - receiver)
    passed = jax.random.randint(jax.random.fold_in(rng, 1), (pairs,), 0, 1 << 20) % (slack + 1)
    lengths = lengths.at[1:1 + 2 * pairs:2].set(giver - passed).at[2:2 + 2 * pairs:2].set(receiver + passed)
    return lengths[jax.random.permutation(jax.random.fold_in(rng, 2), amount)]


def assign_block(own_key, own, number, rows, amount, top, limit, slope):
    order = jax.random.permutation(own_key, amount)
    heavy_load, common = shares(amount, rows * top, limit, slope, True), shares(amount, rows * top, limit, slope, False)
    places = jnp.arange(amount)

    def named(tallies, offset_by):
        used = int((tallies > 0).sum())
        fixed = max(1, used // 4)
        shifted = fixed + (places - fixed + offset_by * (used - fixed)) % max(1, amount - fixed)
        return jnp.zeros((amount,), jnp.int32).at[order[jnp.where(places < fixed, places, shifted)]].set(jnp.asarray(tallies, jnp.int32))

    tallies = jnp.where(number % 4 == 0, named(heavy_load, number // 4), named(common, number - number // 4 - 1))
    mixed = jax.random.permutation(jax.random.fold_in(own, 3), amount)
    giver, taker = mixed[0:amount // 2 * 2:2], mixed[1:amount // 2 * 2:2]
    room = jnp.minimum(tallies[giver] - 1, limit - tallies[taker]) // 2
    room = jnp.where((giver == order[0]) | (taker == order[0]) | (tallies[taker] == 0), 0, jnp.maximum(room, 0))
    shifted = jax.random.randint(jax.random.fold_in(own, 4), (amount // 2,), 0, 1 << 20) % (room + 1)
    tallies = tallies.at[giver].add(-shifted).at[taker].add(shifted)
    labels = jnp.searchsorted(jnp.cumsum(tallies), jnp.arange(rows * top), side="right").astype(jnp.int32)
    grid = labels.reshape(top, rows).T
    grid = grid[jax.random.permutation(jax.random.fold_in(own, 1), rows)]
    offset_by = jax.random.randint(jax.random.fold_in(own, 2), (rows, 1), 0, top)
    return jnp.take_along_axis(grid, (jnp.arange(top)[None, :] + offset_by) % top, axis=1)


def shares(number_of, total, most, lean, full):
    weights = [(1 << 20) // math.isqrt(grade ** lean) + 1 for grade in range(1, number_of + 1)]
    largest = most if full else min(most, max(-(-total // number_of), total * weights[0] // sum(weights)))
    least = 1 if total - largest >= number_of - 1 else 0
    holding, spare = [largest] + [least] * (number_of - 1), total - largest - least * (number_of - 1)
    while spare > 0:
        movable = [i for i in range(1, number_of) if holding[i] < largest] or [i for i in range(1, number_of) if holding[i] < most]
        whole, left = sum([weights[i] for i in movable]), spare
        for i in movable:
            addition = min(most - holding[i], max(1, left * weights[i] // whole), spare)
            holding[i] = holding[i] + addition
            spare = spare - addition
    return np.array(holding)


def bell_draw(key, extent, scale, most, split=(), kind=jnp.bfloat16):
    factor_of = level_of(key, extent, split, -0.22, 0.18) if split else 1.0
    drawn = jax.random.normal(key, extent, jnp.float32) * scale * factor_of
    return jnp.minimum(jnp.maximum(drawn, -most), most).astype(kind)


def setup_inputs(seed: int = 0) -> dict:
    arg_keys = jax.random.split(jax.random.key(seed), 6)
    positions = draw_positions(jax.random.fold_in(arg_keys[5], 71), 0)
    strength = bell_draw(arg_keys[1], (ROWS, PROW), 1.0, 6.0, ((0, 32),), jnp.float32)
    destination_keys = jax.random.split(jax.random.fold_in(arg_keys[2], 1), ROWS // ROWS_DEV)
    destination_turns = jax.random.permutation(jax.random.fold_in(arg_keys[2], 3), ROWS // ROWS_DEV)
    destination = jax.vmap(lambda own, number: assign_block(jax.random.fold_in(arg_keys[2], 2), own, number, ROWS_DEV, DEVICES, 1, CAP, 2))(destination_keys, destination_turns).reshape((ROWS, 1))
    tile_index = plant(jax.random.randint(arg_keys[3], (ROWS,), 0, TILES), jax.random.fold_in(arg_keys[3], 1), 0, TILES - 1).astype(jnp.int32)
    particle_count = ragged(arg_keys[4], ROWS, ROWS * PROW * 3 // 4, PROW, 2).astype(jnp.int32)
    return {"positions": positions, "strength": strength, "destination": destination, "tile_index": tile_index, "particle_count": particle_count}


def spline_weight(offset):
    distance = jnp.abs(offset)
    inner_part = 1.0 - 2.5 * distance * distance + 1.5 * distance * distance * distance
    outer_part = 0.5 * (2.0 - distance) * (2.0 - distance) * (1.0 - distance)
    return jnp.where(distance < 1.0, inner_part, jnp.where(distance < 2.0, outer_part, 0.0))

def row_blocks(coords, weights):
    row_count = coords.shape[0]
    row_width = coords.shape[2]
    along_x = spline_weight(coords[:, 0, :, None] - jnp.arange(BX).astype(coords.dtype))
    along_y = spline_weight(coords[:, 1, :, None] - jnp.arange(BY).astype(coords.dtype))
    along_z = spline_weight(coords[:, 2, :, None] - jnp.arange(NZ).astype(coords.dtype))
    planar = weights[:, :, None, None] * along_x[:, :, :, None] * along_y[:, :, None, :]
    planar = planar.reshape(row_count, row_width, BX * BY)
    return jnp.einsum('rpa,rpz->raz', planar, along_z, precision=lax.Precision.HIGHEST)

def reverse_digits(value, levels):
    result = 0
    for position in range(levels):
        result = result * 2 + (value >> position & 1)
    return result

def spectrum_order(devices, length):
    levels = devices.bit_length() - 1
    local_len = length // devices
    return np.array([reverse_digits(owner_idx, levels) + devices * within for owner_idx in range(devices) for within in range(local_len)], dtype=np.int32)

def reference(positions, strength, destination, tile_index, particle_count):
    total_rows = positions.shape[0]
    width_x = NX // N_PX
    width_y = NY // N_PY
    across_y = width_y // BY
    alive_mask = jnp.arange(PROW, dtype=jnp.int32)[None, :] < particle_count[:, None]
    strength_live = jnp.where(alive_mask, strength, jnp.zeros_like(strength))
    target = destination[:, 0]
    tile_row = target // N_PY * (width_x // BX) + tile_index // across_y
    tile_col = target % N_PY * across_y + tile_index % across_y
    flat_tile = (tile_row * (NY // BY) + tile_col).astype(jnp.int32)
    group_rows = math.gcd(total_rows, 256)

    def deposit(carried, number):
        first_row = (number * group_rows).astype(jnp.int32)
        coords = lax.dynamic_slice_in_dim(positions, first_row, group_rows, 0)
        weights = lax.dynamic_slice_in_dim(strength_live, first_row, group_rows, 0)
        places = lax.dynamic_slice_in_dim(flat_tile, first_row, group_rows, 0)
        return (carried.at[places].add(row_blocks(coords, weights)), None)
    initial = jnp.zeros((NX // BX * (NY // BY), BX * BY, NZ), jnp.float32)
    tile_sums, _ = lax.scan(deposit, initial, jnp.arange(total_rows // group_rows, dtype=jnp.int32))
    vort_field = tile_sums.reshape(NX // BX, NY // BY, BX, BY, NZ).transpose(0, 2, 1, 3, 4).reshape(NX, NY, NZ)
    transformed = jnp.fft.fft2(vort_field, axes=(0, 1)) / math.sqrt(NX * NY)
    transformed = transformed[spectrum_order(N_PX, NX)][:, spectrum_order(N_PY, NY)]
    return jnp.stack([jnp.real(transformed), jnp.imag(transformed)]).astype(jnp.float32)
```

```python
import functools
import math

import jax
import jax.numpy as jnp
from jax import lax
from jax.experimental import pallas as pl
from jax.experimental.pallas import tpu as pltpu
from jax.sharding import PartitionSpec as P

NX = 512
NY = 512
NZ = 256
BX = 16
BY = 8
BF = jnp.bfloat16
VMEM = 56 << 20


def spline(offset):
    a = jnp.abs(offset)
    b = jnp.maximum(2.0 - a, 0.0)
    inner = (1.5 * a - 2.5) * (a * a) + 1.0
    outer = (b * b) * (0.5 * b - 0.5)
    return jnp.where(a < 1.0, inner, outer)


def split(v):
    hi = v.astype(BF)
    return hi, (v - hi.astype(jnp.float32)).astype(BF)


def dot_nt(a, b):
    return lax.dot_general(a, b, (((1,), (1,)), ((), ())), preferred_element_type=jnp.float32)


def dot(a, b):
    return jnp.dot(a, b, preferred_element_type=jnp.float32)


def fill(x, y, z, w, part, planar_hi, planar_lo, depth_hi, depth_lo):
    width = x.shape[1]
    ix = lax.broadcasted_iota(jnp.int32, (BX, width), 0).astype(jnp.float32)
    iy = lax.broadcasted_iota(jnp.int32, (BY, width), 0).astype(jnp.float32)
    lanes = slice(part * width, (part + 1) * width)
    wx = spline(x - ix)
    wy = spline(y - iy) * w
    for i in range(0, BX, 2):
        hi, lo = split(jnp.concatenate([wx[i : i + 1] * wy, wx[i + 1 : i + 2] * wy], 0))
        planar_hi[i * BY : (i + 2) * BY, lanes] = hi
        planar_lo[i * BY : (i + 2) * BY, lanes] = lo
    q0 = jnp.floor((z - 1.0) * 0.0625)
    zr = z - 16.0 * q0
    first_hi, first_lo = split(spline(zr - ix))
    next_hi, next_lo = split(spline(zr - 16.0 - ix))
    block = jnp.broadcast_to(q0, (16, width)).astype(BF)
    zero = jnp.zeros((16, width), BF)
    before = None
    for q in range(NZ // 16):
        here = block == BF(q)
        hi, lo = zero, zero
        if before is not None:
            hi, lo = jnp.where(before, next_hi, hi), jnp.where(before, next_lo, lo)
        depth_hi[q * 16 : q * 16 + 16, lanes] = jnp.where(here, first_hi, hi)
        depth_lo[q * 16 : q * 16 + 16, lanes] = jnp.where(here, first_lo, lo)
        before = here


def deposit_kernel(start, order, data, coef, own, other, acc, *bufs, classes, ch, first):
    tile = (first + pl.program_id(0)) * pl.num_programs(1) + pl.program_id(1)
    width = data.shape[1] // 4
    acc[...] = jnp.zeros_like(acc)
    starts = [start[tile * classes + c] for c in range(classes + 1)]
    bounds = [jnp.int32(0)]
    for c in range(classes):
        bounds.append(bounds[-1] + (starts[c + 1] - starts[c] + ch - 1) // ch)
    total = bounds[classes]
    sets = (bufs[:4], bufs[4:])

    def place(i):
        c, base, s, e = jnp.int32(0), bounds[0], starts[0], starts[1]
        for k in range(1, classes):
            past = i >= bounds[k]
            c = jnp.where(past, k, c)
            base = jnp.where(past, bounds[k], base)
            s = jnp.where(past, starts[k], s)
            e = jnp.where(past, starts[k + 1], e)
        return c, s + (i - base) * ch, e

    def make(i, which):
        _, j0, e = place(i)
        for u in range(ch):
            entry = order[jnp.minimum(j0 + u, order.shape[0] - 1)]
            sign = jnp.where(j0 + u < e, (1 - 2 * (entry & 1)).astype(jnp.float32), 0.0)
            row = data[pl.ds(entry >> 1, 1), :]
            x, y, z, w = (row[:, k * width : (k + 1) * width] for k in range(4))
            fill(x, y, z, w * sign, u, *sets[which])

    def multiply(i, which):
        c, _, _ = place(i)
        planar_hi, planar_lo, depth_hi, depth_lo = (r[...] for r in sets[which])
        both = dot_nt(jnp.concatenate([planar_hi, planar_lo], 0), depth_hi)
        cells = planar_hi.shape[0]
        acc[c] += both[:cells] + both[cells:] + dot_nt(planar_hi, depth_lo)

    make(jnp.int32(0), 0)

    def step(k, _):
        multiply(2 * k, 0)
        make(2 * k + 1, 1)
        multiply(2 * k + 1, 1)
        make(2 * k + 2, 0)
        return 0

    lax.fori_loop(0, (total + 1) // 2, step, 0)
    for k, ref in ((0, own), (2, other)):
        for m in range(2):
            v = coef[(k + m) * classes] * acc[0]
            for c in range(1, classes):
                v = v + coef[(k + m) * classes + c] * acc[c]
            ref[m] = v.reshape(BX, BY, NZ)


def deposit(start, order, data, coef, first, tiles_x, tiles_y, classes, ch):
    rows, lanes = data.shape
    width = lanes // 4
    spec = lambda: pl.BlockSpec((2, BX, BY, NZ), lambda i, j, *_: (0, i, j, 0))
    shape = jax.ShapeDtypeStruct((2, tiles_x * BX, tiles_y * BY, NZ), jnp.float32)
    buffers = [
        pltpu.VMEM((BX * BY, ch * width), BF),
        pltpu.VMEM((BX * BY, ch * width), BF),
        pltpu.VMEM((NZ, ch * width), BF),
        pltpu.VMEM((NZ, ch * width), BF),
    ]
    flops = 6 * rows * BX * BY * NZ * width * tiles_x // 8
    return pl.pallas_call(
        functools.partial(deposit_kernel, classes=classes, ch=ch, first=first),
        grid_spec=pltpu.PrefetchScalarGridSpec(
            num_scalar_prefetch=2,
            grid=(tiles_x, tiles_y),
            in_specs=[
                pl.BlockSpec((rows, lanes), lambda i, j, *_: (0, 0), pipeline_mode=pl.Buffered(1)),
                pl.BlockSpec(memory_space=pltpu.SMEM),
            ],
            out_specs=[spec(), spec()],
            scratch_shapes=[pltpu.VMEM((classes, BX * BY, NZ), jnp.float32)] + buffers + buffers,
        ),
        out_shape=[shape, shape],
        compiler_params=pltpu.CompilerParams(vmem_limit_bytes=VMEM),
        cost_estimate=pl.CostEstimate(flops=flops, bytes_accessed=rows * lanes * 4, transcendentals=0),
    )(start, order, data, coef)


def y_kernel(m2, ml, own, other, out):
    wide = own.shape[2]

    def one(i, _):
        u = jnp.concatenate([own[0, i] + other[0, i], own[1, i] + other[1, i]], 0)
        hi, lo = split(u)
        r = dot(m2[...], jnp.concatenate([hi, lo], 0)) + dot(ml[...], hi)
        out[0, i] = r[:wide]
        out[1, i] = r[wide:]
        return 0

    lax.fori_loop(0, own.shape[1], one, 0, unroll=4)


def y_pass(matrix, own, other):
    hi, lo = matrix
    both = jnp.concatenate([hi, hi], 1)
    _, x, y, z = own.shape
    spec = lambda: pl.BlockSpec((2, BX, y, z), lambda i: (0, i, 0, 0))
    whole = lambda m: pl.BlockSpec(m.shape, lambda i: (0, 0))
    return pl.pallas_call(
        y_kernel,
        grid=(x // BX,),
        in_specs=[whole(both), whole(lo), spec(), spec()],
        out_specs=spec(),
        out_shape=jax.ShapeDtypeStruct(own.shape, jnp.float32),
        compiler_params=pltpu.CompilerParams(vmem_limit_bytes=VMEM),
    )(both, lo, own, other)


def x_kernel(mh, ml, *refs):
    ins, out = refs[:-1], refs[-1]
    wide = out.shape[1]
    for k in range(out.shape[2]):
        hi, lo = split(jnp.concatenate([r[c, :, k, :] for c in range(2) for r in ins], 0))
        r = dot(mh[...], hi) + dot(ml[...], hi) + dot(mh[...], lo)
        out[0, :, k, :] = r[:wide]
        out[1, :, k, :] = r[wide:]


def x_pass(matrix, chunks):
    hi, lo = matrix
    _, _, y, z = chunks[0].shape
    x = sum(c.shape[1] for c in chunks)
    spec = lambda n: pl.BlockSpec((2, n, 8, z), lambda i: (0, 0, i, 0))
    whole = pl.BlockSpec(hi.shape, lambda i: (0, 0))
    return pl.pallas_call(
        x_kernel,
        grid=(y // 8,),
        in_specs=[whole, whole] + [spec(c.shape[1]) for c in chunks],
        out_specs=spec(x),
        out_shape=jax.ShapeDtypeStruct((2, x, y, z), jnp.float32),
        compiler_params=pltpu.CompilerParams(vmem_limit_bytes=VMEM),
    )(hi, lo, *chunks)


def dft_matrix(first, step, cells, total, scale):
    i = jnp.arange(cells, dtype=jnp.int32)
    angle = (2.0 * math.pi / total) * ((first + step * i)[:, None] * i[None, :] % total).astype(jnp.float32)
    c, s = jnp.cos(angle) * scale, jnp.sin(angle) * scale
    m = jnp.concatenate([jnp.concatenate([c, s], 1), jnp.concatenate([-s, c], 1)], 0)
    hi = lax.reduce_precision(m, 8, 7)
    return hi.astype(BF), (m - hi).astype(BF)


def reverse_digits(value, levels):
    result = 0
    for position in range(levels):
        result = result * 2 + ((value >> position) & 1)
    return result


def local(positions, strength, destination, tile_index, particle_count):
    rows, _, width = positions.shape
    n_px, n_py = lax.axis_size("px"), lax.axis_size("py")
    me_x, me_y = lax.axis_index("px"), lax.axis_index("py")
    width_x, width_y = NX // n_px, NY // n_py
    tiles_x, tiles_y = width_x // BX, width_y // BY
    tiles = tiles_x * tiles_y
    assert n_py >= 2 * n_px
    classes = n_py // 2
    res_x = reverse_digits(me_x, n_px.bit_length() - 1)
    res_y = reverse_digits(me_y, n_py.bit_length() - 1)
    side = me_y & 1
    low_y = res_y % classes

    alive = jnp.arange(width, dtype=jnp.int32)[None, :] < particle_count[:, None]
    live = jnp.where(alive, strength, jnp.zeros_like(strength))
    packed = jnp.concatenate([positions.reshape(rows, 3 * width), live], 1)
    info = destination[:, 0] * tiles + tile_index
    groups = [list(range(0, n_py, 2)), list(range(1, n_py, 2))]

    def gather(v):
        v = lax.all_gather(v, "px", tiled=True)
        return lax.all_gather(v, "py", axis_index_groups=groups, tiled=True)

    info = gather(info)
    data = gather(packed)
    total = info.shape[0]

    pencil, tile = info // tiles, info % tiles
    at_x, at_y = pencil // n_py, pencil % n_py
    k = (res_x * at_x * (n_py // n_px) + low_y * at_y) % n_py
    half = k % classes
    group = tile * classes + (half - (half & 1)) + (at_y & 1)
    number = jnp.arange(total, dtype=jnp.int32)
    code = group * (2 * total) + number * 2 + (k >= classes).astype(jnp.int32)
    code = lax.sort(code)
    edges = jnp.arange(tiles * classes + 1, dtype=jnp.int32) * (2 * total)
    start = jnp.sum((code[None, :] < edges[:, None]).astype(jnp.int32), axis=1)
    order = code % (2 * total)

    c = jnp.arange(classes, dtype=jnp.int32)
    odd = c & 1
    exponent = jnp.where(low_y % 2 == 1, c, c - odd).astype(jnp.float32) * (2.0 * math.pi / n_py)
    flip = lambda s: (1 - 2 * (odd * s)).astype(jnp.float32)
    real, imag = jnp.cos(exponent), -jnp.sin(exponent)
    coef = jnp.concatenate([real * flip(side), imag * flip(side), real * flip(1 - side), imag * flip(1 - side)])

    matrix_y = dft_matrix(res_y, n_py, width_y, NY, 1.0 / math.sqrt(NX * NY))
    matrix_x = dft_matrix(res_x, n_px, width_x, NX, 1.0)
    swap = [(i, i ^ 1) for i in range(n_py)]
    parts = 4
    each = tiles_x // parts
    halves = []
    for i in range(parts):
        own, other = deposit(start, order, data, coef, i * each, each, tiles_y, classes, 4)
        halves.append((own, lax.ppermute(other, "py", swap)))
    return x_pass(matrix_x, [y_pass(matrix_y, own, got) for own, got in halves])


def solution(mesh):
    placed = (
        P(("px", "py"), None, None),
        P(("px", "py"), None),
        P(("px", "py"), None),
        P(("px", "py")),
        P(("px", "py")),
    )
    return jax.shard_map(
        local, mesh=mesh, in_specs=placed, out_specs=P(None, "px", "py", None), check_vma=False
    )
```

```python
import functools
import math

import jax
import jax.numpy as jnp
from jax import lax
from jax.experimental import pallas as pl
from jax.experimental.pallas import tpu as pltpu
from jax.sharding import PartitionSpec as P

NX = 512
NY = 512
NZ = 256
BX = 16
BY = 8
BF = jnp.bfloat16
VMEM = 56 << 20
STEP_ROWS = 4
PAIR = 2
DEPTH = 6
LANES = 128


def spline(offset):
    a = jnp.abs(offset)
    b = jnp.maximum(2.0 - a, 0.0)
    inner = (1.5 * a - 2.5) * (a * a) + 1.0
    outer = (b * b) * (0.5 * b - 0.5)
    return jnp.where(a < 1.0, inner, outer)


def split(v):
    hi = v.astype(BF)
    return hi, (v - hi.astype(jnp.float32)).astype(BF)


def dot(a, b):
    return jnp.dot(a, b, preferred_element_type=jnp.float32)


def fill(x, y, z, w, part, planar_hi, planar_lo, depth_hi, depth_lo):
    width = x.shape[1]
    ix = lax.broadcasted_iota(jnp.int32, (BX, width), 0).astype(jnp.float32)
    iy = lax.broadcasted_iota(jnp.int32, (BY, width), 0).astype(jnp.float32)
    lanes = slice(part * width, (part + 1) * width)
    wx = spline(x - ix)
    wy = spline(y - iy) * w
    for i in range(0, BX, 2):
        hi, lo = split(jnp.concatenate([wx[i : i + 1] * wy, wx[i + 1 : i + 2] * wy], 0))
        planar_hi[i * BY : (i + 2) * BY, lanes] = hi
        planar_lo[i * BY : (i + 2) * BY, lanes] = lo
    q0 = jnp.floor((z - 1.0) * 0.0625)
    away = (z - 16.0 * q0) - ix
    far = away > 8.0
    hi, lo = split(spline(jnp.where(far, away - 16.0, away)))
    block = jnp.where(far, q0 + 1.0, q0).astype(BF)
    spread = lambda v: jnp.concatenate([v] * (LANES // 16), 0).T
    hi, lo, block = spread(hi), spread(lo), spread(block)
    zero = jnp.zeros((width, LANES), BF)
    column_block = (lax.broadcasted_iota(jnp.int32, (width, LANES), 1) // 16).astype(jnp.float32)
    for t in range(NZ // LANES):
        here = block == (column_block + float(t * (LANES // 16))).astype(BF)
        depth_hi[lanes, t * LANES : (t + 1) * LANES] = jnp.where(here, hi, zero)
        depth_lo[lanes, t * LANES : (t + 1) * LANES] = jnp.where(here, lo, zero)


def deposit_kernel(
    groups_of, firsts, ends, order, span, coef, *refs, classes, ch, depth, first, blocks
):
    parts, (own, other, acc, data, arrived), bufs = refs[:blocks], refs[blocks : blocks + 5], refs[blocks + 5 :]
    tile = pl.program_id(0) * pl.num_programs(1) + pl.program_id(1)
    width = data.shape[1] // 4
    base = first * pl.num_programs(1) * classes
    sets = [bufs[4 * k : 4 * k + 4] for k in range(depth)]

    def make(t, which):
        t = jnp.minimum(t, groups_of.shape[0] - 1)
        j0, e = firsts[t], ends[t]
        for u in range(ch):
            entry = order[jnp.minimum(j0 + u, order.shape[0] - 1)]
            sign = jnp.where(j0 + u < e, (1 - 2 * (entry & 1)).astype(jnp.float32), 0.0)
            row = data[pl.ds(entry >> 1, 1), :]
            x, y, z, w = (row[:, k * width : (k + 1) * width] for k in range(4))
            fill(x, y, z, w * sign, u, *sets[which])

    def multiply(t, which, stop):
        g = jnp.where(t < stop, groups_of[jnp.minimum(t, groups_of.shape[0] - 1)] - base, acc.shape[0] - 1)
        planar_hi, planar_lo, depth_hi, depth_lo = (r[...] for r in sets[which])
        cells = planar_hi.shape[0]
        v = acc[g]
        for u in range(0, ch, PAIR):
            lanes = slice(u * width, (u + PAIR) * width)
            both = dot(jnp.concatenate([planar_hi[:, lanes], planar_lo[:, lanes]], 0), depth_hi[lanes])
            v = v + (both[:cells] + both[cells:] + dot(planar_hi[:, lanes], depth_lo[lanes]))
        acc[g] = v

    @pl.when(tile == 0)
    def _():
        copies, at = [], 0
        for k, part in enumerate(parts):
            rows = part.shape[0]
            copies.append(pltpu.make_async_copy(part, data.at[at : at + rows], arrived.at[k]))
            at += rows
        for copy in copies:
            copy.start()

        def clear(i, _):
            acc[i] = jnp.zeros(acc.shape[1:], jnp.float32)
            return 0

        lax.fori_loop(0, acc.shape[0], clear, 0)
        for copy in copies:
            copy.wait()
        begin, stop = span[first], span[first + pl.num_programs(0)]
        for k in range(depth):
            make(begin + k, k)

        def step(i, _):
            for k in range(depth):
                t = begin + i * depth + k
                multiply(t, k, stop)
                make(t + depth, k)
            return 0

        lax.fori_loop(0, (stop - begin + depth - 1) // depth, step, 0)

    for k, ref in ((0, own), (2, other)):
        for m in range(2):
            v = coef[(k + m) * classes] * acc[tile * classes]
            for c in range(1, classes):
                v = v + coef[(k + m) * classes + c] * acc[tile * classes + c]
            ref[m] = v.reshape(BX, BY, NZ)


def deposit(plan, blocks, coef, first, tiles_x, tiles_y, classes, ch, depth):
    rows, lanes = sum(b.shape[0] for b in blocks), blocks[0].shape[1]
    width = lanes // 4
    spec = lambda: pl.BlockSpec((2, BX, BY, NZ), lambda i, j, *_: (0, i, j, 0))
    shape = jax.ShapeDtypeStruct((2, tiles_x * BX, tiles_y * BY, NZ), jnp.float32)
    buffers = [
        pltpu.VMEM((BX * BY, ch * width), BF),
        pltpu.VMEM((BX * BY, ch * width), BF),
        pltpu.VMEM((ch * width, NZ), BF),
        pltpu.VMEM((ch * width, NZ), BF),
    ]
    flops = 6 * rows * BX * BY * NZ * width * tiles_x // 8
    return pl.pallas_call(
        functools.partial(deposit_kernel, classes=classes, ch=ch, depth=depth, first=first, blocks=len(blocks)),
        grid_spec=pltpu.PrefetchScalarGridSpec(
            num_scalar_prefetch=5,
            grid=(tiles_x, tiles_y),
            in_specs=[pl.BlockSpec(memory_space=pltpu.SMEM)] + [pl.BlockSpec(memory_space=pl.ANY)] * len(blocks),
            out_specs=[spec(), spec()],
            scratch_shapes=[
                pltpu.VMEM((tiles_x * tiles_y * classes + 1, BX * BY, NZ), jnp.float32),
                pltpu.VMEM((rows, lanes), jnp.float32),
                pltpu.SemaphoreType.DMA((len(blocks),)),
            ]
            + buffers * depth,
        ),
        out_shape=[shape, shape],
        compiler_params=pltpu.CompilerParams(vmem_limit_bytes=VMEM),
        cost_estimate=pl.CostEstimate(flops=flops, bytes_accessed=rows * lanes * 4, transcendentals=0),
    )(*plan, coef, *blocks)


def make_plan(code, radix, group_count, span_groups, ch):
    total = code.shape[0]
    edges = jnp.arange(group_count + 1, dtype=jnp.int32) * radix
    start = jnp.sum((code[None, :] < edges[:, None]).astype(jnp.int32), axis=1)
    steps = (start[1:] - start[:-1] + ch - 1) // ch
    before = jnp.sum(jnp.where(jnp.tri(group_count, k=-1, dtype=jnp.bool_), steps[None, :], 0), axis=1)
    after = before + steps
    t = jnp.arange(total // ch + group_count, dtype=jnp.int32)[:, None]
    mine = (before[None, :] <= t) & (t < after[None, :])
    pick = lambda v: jnp.sum(jnp.where(mine, v, 0), axis=1)
    group = pick(jnp.arange(group_count, dtype=jnp.int32)[None, :])
    first = pick(start[None, :-1] + (t - before[None, :]) * ch)
    end = pick(jnp.broadcast_to(start[None, 1:], mine.shape))
    span = jnp.concatenate([before[::span_groups], after[-1:]])
    return group, first, end, code % radix, span


def y_kernel(m2, ml, own, other, out):
    wide = own.shape[2]

    def one(i, _):
        u = jnp.concatenate([own[0, i] + other[0, i], own[1, i] + other[1, i]], 0)
        hi, lo = split(u)
        r = dot(m2[...], jnp.concatenate([hi, lo], 0)) + dot(ml[...], hi)
        out[0, i] = r[:wide]
        out[1, i] = r[wide:]
        return 0

    lax.fori_loop(0, own.shape[1], one, 0, unroll=4)


def y_pass(matrix, own, other):
    hi, lo = matrix
    both = jnp.concatenate([hi, hi], 1)
    _, x, y, z = own.shape
    spec = lambda: pl.BlockSpec((2, BX, y, z), lambda i: (0, i, 0, 0))
    whole = lambda m: pl.BlockSpec(m.shape, lambda i: (0, 0))
    return pl.pallas_call(
        y_kernel,
        grid=(x // BX,),
        in_specs=[whole(both), whole(lo), spec(), spec()],
        out_specs=spec(),
        out_shape=jax.ShapeDtypeStruct(own.shape, jnp.float32),
        compiler_params=pltpu.CompilerParams(vmem_limit_bytes=VMEM),
    )(both, lo, own, other)


def x_kernel(mh, ml, *refs):
    ins, out = refs[:-1], refs[-1]
    wide = out.shape[1]
    for k in range(out.shape[2]):
        hi, lo = split(jnp.concatenate([r[c, :, k, :] for c in range(2) for r in ins], 0))
        r = dot(mh[...], hi) + dot(ml[...], hi) + dot(mh[...], lo)
        out[0, :, k, :] = r[:wide]
        out[1, :, k, :] = r[wide:]


def x_pass(matrix, chunks):
    hi, lo = matrix
    _, _, y, z = chunks[0].shape
    x = sum(c.shape[1] for c in chunks)
    spec = lambda n: pl.BlockSpec((2, n, 8, z), lambda i: (0, 0, i, 0))
    whole = pl.BlockSpec(hi.shape, lambda i: (0, 0))
    return pl.pallas_call(
        x_kernel,
        grid=(y // 8,),
        in_specs=[whole, whole] + [spec(c.shape[1]) for c in chunks],
        out_specs=spec(x),
        out_shape=jax.ShapeDtypeStruct((2, x, y, z), jnp.float32),
        compiler_params=pltpu.CompilerParams(vmem_limit_bytes=VMEM),
    )(hi, lo, *chunks)


def dft_matrix(first, step, cells, total, scale):
    i = jnp.arange(cells, dtype=jnp.int32)
    angle = (2.0 * math.pi / total) * ((first + step * i)[:, None] * i[None, :] % total).astype(jnp.float32)
    c, s = jnp.cos(angle) * scale, jnp.sin(angle) * scale
    m = jnp.concatenate([jnp.concatenate([c, s], 1), jnp.concatenate([-s, c], 1)], 0)
    hi = lax.reduce_precision(m, 8, 7)
    return hi.astype(BF), (m - hi).astype(BF)


def reverse_digits(value, levels):
    result = 0
    for position in range(levels):
        result = result * 2 + ((value >> position) & 1)
    return result


def gather_rows(v, tail, n_px, n_py, side):
    rows = v.shape[0] - tail
    if n_py != 8:
        groups = [list(range(0, n_py, 2)), list(range(1, n_py, 2))]
        got = lax.all_gather(lax.all_gather(v, "px", tiled=True), "py", axis_index_groups=groups, tiled=True)
        return [got], got.reshape(-1, rows + tail, v.shape[1])[:, rows:]
    flip = lambda u, axis, n, m: lax.ppermute(u, axis, [(i, i ^ m) for i in range(n)])
    half = rows // 2
    blocks, tails = [], []
    for u in [v] + [flip(v, "px", n_px, m) for m in range(1, n_px)]:
        one, two = flip(u, "py", n_py, 2), flip(u, "py", n_py, 4)
        rest = flip(two[half:], "py", n_py, 2)
        blocks += [u, one, two, flip(one[:half], "py", n_py, 4), rest]
        tails += [u[rows:], one[rows:], two[rows:], rest[rows - half :]]
    return blocks, jnp.stack(tails)


def local(positions, strength, destination, tile_index, particle_count):
    rows, _, width = positions.shape
    n_px, n_py = lax.axis_size("px"), lax.axis_size("py")
    me_x, me_y = lax.axis_index("px"), lax.axis_index("py")
    width_x, width_y = NX // n_px, NY // n_py
    tiles_x, tiles_y = width_x // BX, width_y // BY
    tiles = tiles_x * tiles_y
    assert n_py >= 2 * n_px
    classes = n_py // 2
    res_x = reverse_digits(me_x, n_px.bit_length() - 1)
    res_y = reverse_digits(me_y, n_py.bit_length() - 1)
    side = me_y & 1
    low_y = res_y % classes

    alive = jnp.arange(width, dtype=jnp.int32)[None, :] < particle_count[:, None]
    live = jnp.where(alive, strength, jnp.zeros_like(strength))
    packed = jnp.concatenate([positions.reshape(rows, 3 * width), live], 1)
    info = (destination[:, 0] * tiles + tile_index).astype(jnp.float32)
    tail = -(-rows // (4 * width) // 8) * 8
    info = jnp.pad(info, (0, tail * 4 * width - rows)).reshape(tail, 4 * width)
    blocks, tails = gather_rows(jnp.concatenate([packed, info], 0), tail, n_px, n_py, me_y & 1)
    info = tails.reshape(tails.shape[0], -1)[:, :rows].astype(jnp.int32)
    number = jnp.arange(info.shape[0], dtype=jnp.int32)[:, None] * (rows + tail) + jnp.arange(rows, dtype=jnp.int32)
    radix = 2 * info.shape[0] * (rows + tail)

    pencil, tile = info // tiles, info % tiles
    at_x, at_y = pencil // n_py, pencil % n_py
    k = (res_x * at_x * (n_py // n_px) + low_y * at_y) % n_py
    half = k % classes
    group = tile * classes + (half - (half & 1)) + (at_y & 1)
    code = group * radix + number * 2 + (k >= classes).astype(jnp.int32)
    plan = make_plan(lax.sort(code.reshape(-1)), radix, tiles * classes, tiles_y * classes, STEP_ROWS)

    c = jnp.arange(classes, dtype=jnp.int32)
    odd = c & 1
    exponent = jnp.where(low_y % 2 == 1, c, c - odd).astype(jnp.float32) * (2.0 * math.pi / n_py)
    flip = lambda s: (1 - 2 * (odd * s)).astype(jnp.float32)
    real, imag = jnp.cos(exponent), -jnp.sin(exponent)
    coef = jnp.concatenate([real * flip(side), imag * flip(side), real * flip(1 - side), imag * flip(1 - side)])

    matrix_y = dft_matrix(res_y, n_py, width_y, NY, 1.0 / math.sqrt(NX * NY))
    matrix_x = dft_matrix(res_x, n_px, width_x, NX, 1.0)
    swap = [(i, i ^ 1) for i in range(n_py)]
    last = max(1, tiles_x // 4)
    halves = []
    for first, each in ((0, tiles_x - last), (tiles_x - last, last)):
        own, other = deposit(plan, blocks, coef, first, each, tiles_y, classes, STEP_ROWS, DEPTH)
        halves.append((own, lax.ppermute(other, "py", swap)))
    return x_pass(matrix_x, [y_pass(matrix_y, own, got) for own, got in halves])


def solution(mesh):
    placed = (
        P(("px", "py"), None, None),
        P(("px", "py"), None),
        P(("px", "py"), None),
        P(("px", "py")),
        P(("px", "py")),
    )
    return jax.shard_map(
        local, mesh=mesh, in_specs=placed, out_specs=P(None, "px", "py", None), check_vma=False
    )
```

```python
import functools
import math

import jax
import jax.numpy as jnp
from jax import lax
from jax.experimental import pallas as pl
from jax.experimental.pallas import tpu as pltpu
from jax.sharding import PartitionSpec as P

NX = 512
NY = 512
NZ = 256
BX = 16
BY = 8
BF = jnp.bfloat16
VMEM = 56 << 20
STEP_ROWS = 2
PAIR = 2
DEPTH = 32
LANES = 128


def spline(offset):
    a = jnp.abs(offset)
    b = jnp.maximum(2.0 - a, 0.0)
    inner = (1.5 * a - 2.5) * (a * a) + 1.0
    outer = (b * b) * (0.5 * b - 0.5)
    return jnp.where(a < 1.0, inner, outer)


def split(v):
    hi = v.astype(BF)
    return hi, (v - hi.astype(jnp.float32)).astype(BF)


def dot(a, b):
    return jnp.dot(a, b, preferred_element_type=jnp.float32)


def fill(x, y, z, w):
    width = x.shape[1]
    ix = lax.broadcasted_iota(jnp.int32, (BX, width), 0).astype(jnp.float32)
    iy = lax.broadcasted_iota(jnp.int32, (BY, width), 0).astype(jnp.float32)
    wx = spline(x - ix)
    wy = spline(y - iy) * w
    planar_hi, planar_lo, depth_hi, depth_lo = [], [], [], []
    for i in range(0, BX, 2):
        hi, lo = split(jnp.concatenate([wx[i : i + 1] * wy, wx[i + 1 : i + 2] * wy], 0))
        planar_hi.append(hi)
        planar_lo.append(lo)
    q0 = jnp.floor((z - 1.0) * 0.0625)
    away = (z - 16.0 * q0) - ix
    far = away > 8.0
    hi, lo = split(spline(jnp.where(far, away - 16.0, away)))
    block = jnp.where(far, q0 + 1.0, q0).astype(BF)
    spread = lambda v: jnp.concatenate([v] * (LANES // 16), 0).T
    hi, lo, block = spread(hi), spread(lo), spread(block)
    zero = jnp.zeros((width, LANES), BF)
    column_block = (lax.broadcasted_iota(jnp.int32, (width, LANES), 1) // 16).astype(jnp.float32)
    for t in range(NZ // LANES):
        here = block == (column_block + float(t * (LANES // 16))).astype(BF)
        depth_hi.append(jnp.where(here, hi, zero))
        depth_lo.append(jnp.where(here, lo, zero))
    return [jnp.concatenate(v, 0) for v in (planar_hi, planar_lo)] + [jnp.concatenate(v, 1) for v in (depth_hi, depth_lo)]


def deposit_kernel(
    groups_of, firsts, ends, order, span, coef, *refs, classes, ch, depth, first, blocks
):
    parts, (own, other, acc, data, arrived) = refs[:blocks], refs[blocks:]
    tile = pl.program_id(0) * pl.num_programs(1) + pl.program_id(1)
    width = data.shape[1] // 4
    base = first * pl.num_programs(1) * classes

    def multiply(t, stop):
        live = t < stop
        t = jnp.minimum(t, groups_of.shape[0] - 1)
        j0, e = firsts[t], jnp.where(live, ends[t], 0)
        g = jnp.where(live, groups_of[t] - base, acc.shape[0] - 1)
        v = None
        for u in range(0, ch, PAIR):
            made = []
            for j in range(u, u + PAIR):
                entry = order[jnp.minimum(j0 + j, order.shape[0] - 1)]
                sign = jnp.where(j0 + j < e, (1 - 2 * (entry & 1)).astype(jnp.float32), 0.0)
                row = data[pl.ds(entry >> 1, 1), :]
                x, y, z, w = (row[:, k * width : (k + 1) * width] for k in range(4))
                made.append(fill(x, y, z, w * sign))
            ph, plo = (jnp.concatenate([m[k] for m in made], 1) for k in range(2))
            dh, dl = (jnp.concatenate([m[k] for m in made], 0) for k in range(2, 4))
            cells = ph.shape[0]
            both = dot(jnp.concatenate([ph, plo], 0), dh)
            p = both[:cells] + both[cells:] + dot(ph, dl)
            v = p if v is None else v + p
        acc[g] += v

    @pl.when(tile == 0)
    def _():
        copies, at = [], 0
        for k, part in enumerate(parts):
            rows = part.shape[0]
            copies.append(pltpu.make_async_copy(part, data.at[at : at + rows], arrived.at[k]))
            at += rows
        for copy in copies:
            copy.start()

        def clear(i, _):
            acc[i] = jnp.zeros(acc.shape[1:], jnp.float32)
            return 0

        lax.fori_loop(0, acc.shape[0], clear, 0)
        for copy in copies:
            copy.wait()
        begin, stop = span[first], span[first + pl.num_programs(0)]

        def step(i, _):
            for k in range(depth):
                t = begin + i * depth + k
                multiply(t, stop)
            return 0

        lax.fori_loop(0, (stop - begin + depth - 1) // depth, step, 0)

    for k, ref in ((0, own), (2, other)):
        for m in range(2):
            v = coef[(k + m) * classes] * acc[tile * classes]
            for c in range(1, classes):
                v = v + coef[(k + m) * classes + c] * acc[tile * classes + c]
            ref[m] = v.reshape(BX, BY, NZ)


def deposit(plan, blocks, coef, first, tiles_x, tiles_y, classes, ch, depth):
    rows, lanes = sum(b.shape[0] for b in blocks), blocks[0].shape[1]
    width = lanes // 4
    spec = lambda: pl.BlockSpec((2, BX, BY, NZ), lambda i, j, *_: (0, i, j, 0))
    shape = jax.ShapeDtypeStruct((2, tiles_x * BX, tiles_y * BY, NZ), jnp.float32)
    flops = 6 * rows * BX * BY * NZ * width * tiles_x // 8
    return pl.pallas_call(
        functools.partial(deposit_kernel, classes=classes, ch=ch, depth=depth, first=first, blocks=len(blocks)),
        grid_spec=pltpu.PrefetchScalarGridSpec(
            num_scalar_prefetch=5,
            grid=(tiles_x, tiles_y),
            in_specs=[pl.BlockSpec(memory_space=pltpu.SMEM)] + [pl.BlockSpec(memory_space=pl.ANY)] * len(blocks),
            out_specs=[spec(), spec()],
            scratch_shapes=[
                pltpu.VMEM((tiles_x * tiles_y * classes + 1, BX * BY, NZ), jnp.float32),
                pltpu.VMEM((rows, lanes), jnp.float32),
                pltpu.SemaphoreType.DMA((len(blocks),)),
            ],
        ),
        out_shape=[shape, shape],
        compiler_params=pltpu.CompilerParams(vmem_limit_bytes=VMEM),
        cost_estimate=pl.CostEstimate(flops=flops, bytes_accessed=rows * lanes * 4, transcendentals=0),
    )(*plan, coef, *blocks)


def make_plan(code, radix, group_count, span_groups, ch):
    total = code.shape[0]
    edges = jnp.arange(group_count + 1, dtype=jnp.int32) * radix
    start = jnp.sum((code[None, :] < edges[:, None]).astype(jnp.int32), axis=1)
    steps = (start[1:] - start[:-1] + ch - 1) // ch
    before = jnp.sum(jnp.where(jnp.tri(group_count, k=-1, dtype=jnp.bool_), steps[None, :], 0), axis=1)
    after = before + steps
    t = jnp.arange(total // ch + group_count, dtype=jnp.int32)[:, None]
    mine = (before[None, :] <= t) & (t < after[None, :])
    pick = lambda v: jnp.sum(jnp.where(mine, v, 0), axis=1)
    group = pick(jnp.arange(group_count, dtype=jnp.int32)[None, :])
    first = pick(start[None, :-1] + (t - before[None, :]) * ch)
    end = pick(jnp.broadcast_to(start[None, 1:], mine.shape))
    span = jnp.concatenate([before[::span_groups], after[-1:]])
    return group, first, end, code % radix, span


def y_kernel(m2, ml, own, other, out):
    wide = own.shape[2]

    def one(i, _):
        u = jnp.concatenate([own[0, i] + other[0, i], own[1, i] + other[1, i]], 0)
        hi, lo = split(u)
        r = dot(m2[...], jnp.concatenate([hi, lo], 0)) + dot(ml[...], hi)
        out[0, i] = r[:wide]
        out[1, i] = r[wide:]
        return 0

    lax.fori_loop(0, own.shape[1], one, 0, unroll=4)


def y_pass(matrix, own, other):
    hi, lo = matrix
    both = jnp.concatenate([hi, hi], 1)
    _, x, y, z = own.shape
    spec = lambda: pl.BlockSpec((2, BX, y, z), lambda i: (0, i, 0, 0))
    whole = lambda m: pl.BlockSpec(m.shape, lambda i: (0, 0))
    return pl.pallas_call(
        y_kernel,
        grid=(x // BX,),
        in_specs=[whole(both), whole(lo), spec(), spec()],
        out_specs=spec(),
        out_shape=jax.ShapeDtypeStruct(own.shape, jnp.float32),
        compiler_params=pltpu.CompilerParams(vmem_limit_bytes=VMEM),
        cost_estimate=pl.CostEstimate(flops=24 * x * y * y * z, bytes_accessed=24 * x * y * z, transcendentals=0),
    )(both, lo, own, other)


def x_kernel(mh, ml, *refs):
    ins, out = refs[:-1], refs[-1]
    wide = out.shape[1]
    for k in range(out.shape[2]):
        hi, lo = split(jnp.concatenate([r[c, :, k, :] for c in range(2) for r in ins], 0))
        r = dot(mh[...], hi) + dot(ml[...], hi) + dot(mh[...], lo)
        out[0, :, k, :] = r[:wide]
        out[1, :, k, :] = r[wide:]


def x_pass(matrix, chunks):
    hi, lo = matrix
    _, _, y, z = chunks[0].shape
    x = sum(c.shape[1] for c in chunks)
    spec = lambda n: pl.BlockSpec((2, n, 8, z), lambda i: (0, 0, i, 0))
    whole = pl.BlockSpec(hi.shape, lambda i: (0, 0))
    return pl.pallas_call(
        x_kernel,
        grid=(y // 8,),
        in_specs=[whole, whole] + [spec(c.shape[1]) for c in chunks],
        out_specs=spec(x),
        out_shape=jax.ShapeDtypeStruct((2, x, y, z), jnp.float32),
        compiler_params=pltpu.CompilerParams(vmem_limit_bytes=VMEM),
    )(hi, lo, *chunks)


def dft_matrix(first, step, cells, total, scale):
    i = jnp.arange(cells, dtype=jnp.int32)
    angle = (2.0 * math.pi / total) * ((first + step * i)[:, None] * i[None, :] % total).astype(jnp.float32)
    c, s = jnp.cos(angle) * scale, jnp.sin(angle) * scale
    m = jnp.concatenate([jnp.concatenate([c, s], 1), jnp.concatenate([-s, c], 1)], 0)
    hi = lax.reduce_precision(m, 8, 7)
    return hi.astype(BF), (m - hi).astype(BF)


def reverse_digits(value, levels):
    result = 0
    for position in range(levels):
        result = result * 2 + ((value >> position) & 1)
    return result


def gather_rows(v, tail, n_px, n_py, side):
    rows = v.shape[0] - tail
    if n_py != 8:
        groups = [list(range(0, n_py, 2)), list(range(1, n_py, 2))]
        got = lax.all_gather(lax.all_gather(v, "px", tiled=True), "py", axis_index_groups=groups, tiled=True)
        return [got], got.reshape(-1, rows + tail, v.shape[1])[:, rows:]
    flip = lambda u, axis, n, m: lax.ppermute(u, axis, [(i, i ^ m) for i in range(n)])
    half = rows // 2
    blocks, tails = [], []
    for u in [v] + [flip(v, "px", n_px, m) for m in range(1, n_px)]:
        one, two = flip(u, "py", n_py, 2), flip(u, "py", n_py, 4)
        rest = flip(two[half:], "py", n_py, 2)
        blocks += [u, one, two, flip(one[:half], "py", n_py, 4), rest]
        tails += [u[rows:], one[rows:], two[rows:], rest[rows - half :]]
    return blocks, jnp.stack(tails)


def local(positions, strength, destination, tile_index, particle_count):
    rows, _, width = positions.shape
    n_px, n_py = lax.axis_size("px"), lax.axis_size("py")
    me_x, me_y = lax.axis_index("px"), lax.axis_index("py")
    width_x, width_y = NX // n_px, NY // n_py
    tiles_x, tiles_y = width_x // BX, width_y // BY
    tiles = tiles_x * tiles_y
    assert n_py >= 2 * n_px
    classes = n_py // 2
    res_x = reverse_digits(me_x, n_px.bit_length() - 1)
    res_y = reverse_digits(me_y, n_py.bit_length() - 1)
    side = me_y & 1
    low_y = res_y % classes

    alive = jnp.arange(width, dtype=jnp.int32)[None, :] < particle_count[:, None]
    live = jnp.where(alive, strength, jnp.zeros_like(strength))
    packed = jnp.concatenate([positions.reshape(rows, 3 * width), live], 1)
    info = (destination[:, 0] * tiles + tile_index).astype(jnp.float32)
    tail = -(-rows // (4 * width) // 8) * 8
    info = jnp.pad(info, (0, tail * 4 * width - rows)).reshape(tail, 4 * width)
    blocks, tails = gather_rows(jnp.concatenate([packed, info], 0), tail, n_px, n_py, me_y & 1)
    info = tails.reshape(tails.shape[0], -1)[:, :rows].astype(jnp.int32)
    number = jnp.arange(info.shape[0], dtype=jnp.int32)[:, None] * (rows + tail) + jnp.arange(rows, dtype=jnp.int32)
    radix = 2 * info.shape[0] * (rows + tail)

    pencil, tile = info // tiles, info % tiles
    at_x, at_y = pencil // n_py, pencil % n_py
    k = (res_x * at_x * (n_py // n_px) + low_y * at_y) % n_py
    half = k % classes
    group = tile * classes + (half - (half & 1)) + (at_y & 1)
    code = group * radix + number * 2 + (k >= classes).astype(jnp.int32)
    plan = make_plan(lax.sort(code.reshape(-1)), radix, tiles * classes, tiles_y * classes, STEP_ROWS)

    c = jnp.arange(classes, dtype=jnp.int32)
    odd = c & 1
    exponent = jnp.where(low_y % 2 == 1, c, c - odd).astype(jnp.float32) * (2.0 * math.pi / n_py)
    flip = lambda s: (1 - 2 * (odd * s)).astype(jnp.float32)
    real, imag = jnp.cos(exponent), -jnp.sin(exponent)
    coef = jnp.concatenate([real * flip(side), imag * flip(side), real * flip(1 - side), imag * flip(1 - side)])

    matrix_y = dft_matrix(res_y, n_py, width_y, NY, 1.0 / math.sqrt(NX * NY))
    matrix_x = dft_matrix(res_x, n_px, width_x, NX, 1.0)
    swap = [(i, i ^ 1) for i in range(n_py)]
    last = max(1, tiles_x // 4)
    halves = []
    for first, each in ((0, tiles_x - last), (tiles_x - last, last)):
        own, other = deposit(plan, blocks, coef, first, each, tiles_y, classes, STEP_ROWS, DEPTH)
        halves.append((own, lax.ppermute(other, "py", swap)))
    return x_pass(matrix_x, [y_pass(matrix_y, own, got) for own, got in halves])


def solution(mesh):
    placed = (
        P(("px", "py"), None, None),
        P(("px", "py"), None),
        P(("px", "py"), None),
        P(("px", "py")),
        P(("px", "py")),
    )
    return jax.shard_map(
        local, mesh=mesh, in_specs=placed, out_specs=P(None, "px", "py", None), check_vma=False
    )
```

```python
import functools
import math

import jax
import jax.numpy as jnp
import numpy as np
from jax import lax
from jax.experimental import pallas as pl
from jax.experimental.pallas import tpu as pltpu
from jax.sharding import PartitionSpec as P

NX = 512
NY = 512
NZ = 256
BX = 16
BY = 8
BF = jnp.bfloat16
VMEM = 56 << 20
STEP_ROWS = 2
PAIR = 2
DEPTH = 32
LANES = 128


def spline(offset):
    a = jnp.abs(offset)
    b = jnp.maximum(2.0 - a, 0.0)
    inner = (1.5 * a - 2.5) * (a * a) + 1.0
    outer = (b * b) * (0.5 * b - 0.5)
    return jnp.where(a < 1.0, inner, outer)


def split(v):
    hi = v.astype(BF)
    return hi, (v - hi.astype(jnp.float32)).astype(BF)


def dot(a, b):
    return jnp.dot(a, b, preferred_element_type=jnp.float32)


def fill(x, y, z, w):
    width = x.shape[1]
    ix = lax.broadcasted_iota(jnp.int32, (BX, width), 0).astype(jnp.float32)
    iy = lax.broadcasted_iota(jnp.int32, (BY, width), 0).astype(jnp.float32)
    wx = spline(x - ix)
    wy = spline(y - iy) * w
    planar_hi, planar_lo, depth_hi, depth_lo = [], [], [], []
    for i in range(0, BX, 2):
        hi, lo = split(jnp.concatenate([wx[i : i + 1] * wy, wx[i + 1 : i + 2] * wy], 0))
        planar_hi.append(hi)
        planar_lo.append(lo)
    q0 = jnp.floor((z - 1.0) * 0.0625)
    away = (z - 16.0 * q0) - ix
    far = away > 8.0
    hi, lo = split(spline(jnp.where(far, away - 16.0, away)))
    block = jnp.where(far, q0 + 1.0, q0).astype(BF)
    spread = lambda v: jnp.concatenate([v] * (LANES // 16), 0).T
    hi, lo, block = spread(hi), spread(lo), spread(block)
    zero = jnp.zeros((width, LANES), BF)
    column_block = (lax.broadcasted_iota(jnp.int32, (width, LANES), 1) // 16).astype(jnp.float32)
    for t in range(NZ // LANES):
        here = block == (column_block + float(t * (LANES // 16))).astype(BF)
        depth_hi.append(jnp.where(here, hi, zero))
        depth_lo.append(jnp.where(here, lo, zero))
    return [jnp.concatenate(v, 0) for v in (planar_hi, planar_lo)] + [jnp.concatenate(v, 1) for v in (depth_hi, depth_lo)]


def deposit_kernel(
    groups_of, firsts, ends, order, span, coef, *refs, classes, ch, depth, first, blocks
):
    parts, (own, other, acc, data, arrived) = refs[:blocks], refs[blocks:]
    tile = pl.program_id(0) * pl.num_programs(1) + pl.program_id(1)
    width = data.shape[1] // 4
    base = first * pl.num_programs(1) * classes

    def multiply(t, stop):
        live = t < stop
        t = jnp.minimum(t, groups_of.shape[0] - 1)
        j0, e = firsts[t], jnp.where(live, ends[t], 0)
        g = jnp.where(live, groups_of[t] - base, acc.shape[0] - 1)
        v = None
        for u in range(0, ch, PAIR):
            made = []
            for j in range(u, u + PAIR):
                entry = order[jnp.minimum(j0 + j, order.shape[0] - 1)]
                sign = jnp.where(j0 + j < e, (1 - 2 * (entry & 1)).astype(jnp.float32), 0.0)
                row = data[pl.ds(entry >> 1, 1), :]
                x, y, z, w = (row[:, k * width : (k + 1) * width] for k in range(4))
                made.append(fill(x, y, z, w * sign))
            ph, plo = (jnp.concatenate([m[k] for m in made], 1) for k in range(2))
            dh, dl = (jnp.concatenate([m[k] for m in made], 0) for k in range(2, 4))
            cells = ph.shape[0]
            both = dot(jnp.concatenate([ph, plo], 0), dh)
            p = both[:cells] + both[cells:] + dot(ph, dl)
            v = p if v is None else v + p
        acc[g] += v

    @pl.when(tile == 0)
    def _():
        copies, at = [], 0
        for k, part in enumerate(parts):
            rows = part.shape[0]
            copies.append(pltpu.make_async_copy(part, data.at[at : at + rows], arrived.at[k]))
            at += rows
        for copy in copies:
            copy.start()

        def clear(i, _):
            acc[i] = jnp.zeros(acc.shape[1:], jnp.float32)
            return 0

        lax.fori_loop(0, acc.shape[0], clear, 0)
        for copy in copies:
            copy.wait()
        begin, stop = span[first], span[first + pl.num_programs(0)]

        def step(i, _):
            for k in range(depth):
                t = begin + i * depth + k
                multiply(t, stop)
            return 0

        lax.fori_loop(0, (stop - begin + depth - 1) // depth, step, 0)

    for m in range(2):
        even, odd = (
            functools.reduce(
                jnp.add, [coef[m * classes + c] * acc[tile * classes + c] for c in range(parity, classes, 2)]
            )
            for parity in range(2)
        )
        own[m] = (even + odd).reshape(BX, BY, NZ)
        other[m] = (even - odd).reshape(BX, BY, NZ)


def deposit(plan, blocks, coef, first, tiles_x, tiles_y, classes, ch, depth):
    rows, lanes = sum(b.shape[0] for b in blocks), blocks[0].shape[1]
    width = lanes // 4
    spec = lambda: pl.BlockSpec((2, BX, BY, NZ), lambda i, j, *_: (0, i, j, 0))
    shape = jax.ShapeDtypeStruct((2, tiles_x * BX, tiles_y * BY, NZ), jnp.float32)
    flops = 6 * rows * BX * BY * NZ * width * tiles_x // 8
    return pl.pallas_call(
        functools.partial(deposit_kernel, classes=classes, ch=ch, depth=depth, first=first, blocks=len(blocks)),
        grid_spec=pltpu.PrefetchScalarGridSpec(
            num_scalar_prefetch=5,
            grid=(tiles_x, tiles_y),
            in_specs=[pl.BlockSpec(memory_space=pltpu.SMEM)] + [pl.BlockSpec(memory_space=pl.ANY)] * len(blocks),
            out_specs=[spec(), spec()],
            scratch_shapes=[
                pltpu.VMEM((tiles_x * tiles_y * classes + 1, BX * BY, NZ), jnp.float32),
                pltpu.VMEM((rows, lanes), jnp.float32),
                pltpu.SemaphoreType.DMA((len(blocks),)),
            ],
        ),
        out_shape=[shape, shape],
        compiler_params=pltpu.CompilerParams(vmem_limit_bytes=VMEM),
        cost_estimate=pl.CostEstimate(flops=flops, bytes_accessed=rows * lanes * 4, transcendentals=0),
    )(*plan, coef, *blocks)


def make_plan(code, radix, group_count, span_groups, ch):
    total = code.shape[0]
    edges = jnp.arange(group_count + 1, dtype=jnp.int32) * radix
    start = jnp.sum((code[None, :] < edges[:, None]).astype(jnp.int32), axis=1)
    steps = (start[1:] - start[:-1] + ch - 1) // ch
    before = jnp.sum(jnp.where(jnp.tri(group_count, k=-1, dtype=jnp.bool_), steps[None, :], 0), axis=1)
    after = before + steps
    t = jnp.arange(total // ch + group_count, dtype=jnp.int32)[:, None]
    mine = (before[None, :] <= t) & (t < after[None, :])
    pick = lambda v: jnp.sum(jnp.where(mine, v, 0), axis=1)
    group = pick(jnp.arange(group_count, dtype=jnp.int32)[None, :])
    first = pick(start[None, :-1] + (t - before[None, :]) * ch)
    end = pick(jnp.broadcast_to(start[None, 1:], mine.shape))
    span = jnp.concatenate([before[::span_groups], after[-1:]])
    return group, first, end, code % radix, span


def transform_kernel(yh, yl, xh, xl, *refs, counts):
    out, held = refs[-2:]
    t = pl.program_id(0)
    wide_y, wide_x = held.shape[2], held.shape[1]

    begin = 0
    for n, (own, got) in zip(counts, zip(refs[0:-2:2], refs[1:-2:2])):

        @pl.when((t >= begin) & (t < begin + n))
        def _(own=own, got=got):
            def one(i, _):
                u = jnp.concatenate([own[0, i] + got[0, i], own[1, i] + got[1, i]], 0)
                hi, lo = split(u)
                r = dot(yh[...], jnp.concatenate([hi, lo], 0)) + dot(yl[...], hi)
                held[0, t * BX + i] = r[:wide_y]
                held[1, t * BX + i] = r[wide_y:]
                return 0

            lax.fori_loop(0, BX, one, 0, unroll=8)

        begin += n

    @pl.when(t >= begin)
    def _():
        at = pl.multiple_of((t - begin) * 8, 8)
        u = jnp.concatenate([jnp.swapaxes(held[c, :, pl.ds(at, 8), :], 0, 1) for c in range(2)], 1)
        done = []
        for k in range(8):
            hi, lo = split(u[k])
            done.append(dot(xh[...], hi) + dot(xl[...], hi) + dot(xh[...], lo))
        w = jnp.stack(done)
        out[0] = jnp.swapaxes(w[:, :wide_x], 0, 1)
        out[1] = jnp.swapaxes(w[:, wide_x:], 0, 1)


def transform(matrix_y, matrix_x, halves):
    (yh, yl), (xh, xl) = matrix_y, matrix_x
    yh = jnp.concatenate([yh, yh], 1)
    _, _, y, z = halves[0][0].shape
    counts = [own.shape[1] // BX for own, _ in halves]
    whole = lambda m: pl.BlockSpec(m.shape, lambda t: (0, 0))
    specs, begin = [], 0
    for n in counts:
        spec = pl.BlockSpec((2, BX, y, z), lambda t, n=n, begin=begin: (0, jnp.clip(t - begin, 0, n - 1), 0, 0))
        specs += [spec, spec]
        begin += n
    x = begin * BX
    return pl.pallas_call(
        functools.partial(transform_kernel, counts=counts),
        grid=(begin + y // 8,),
        in_specs=[whole(yh), whole(yl), whole(xh), whole(xl)] + specs,
        out_specs=pl.BlockSpec((2, x, 8, z), lambda t: (0, 0, jnp.maximum(t - begin, 0), 0)),
        out_shape=jax.ShapeDtypeStruct((2, x, y, z), jnp.float32),
        scratch_shapes=[pltpu.VMEM((2, x, y, z), jnp.float32)],
        compiler_params=pltpu.CompilerParams(vmem_limit_bytes=VMEM),
    )(yh, yl, xh, xl, *[v for half in halves for v in half])


def dft_matrix(first, step, cells, total, scale):
    i = jnp.arange(cells, dtype=jnp.int32)
    angle = (2.0 * math.pi / total) * ((first + step * i)[:, None] * i[None, :] % total).astype(jnp.float32)
    c, s = jnp.cos(angle) * scale, jnp.sin(angle) * scale
    m = jnp.concatenate([jnp.concatenate([c, s], 1), jnp.concatenate([-s, c], 1)], 0)
    hi = lax.reduce_precision(m, 8, 7)
    return hi.astype(BF), (m - hi).astype(BF)


def reverse_digits(value, levels):
    result = 0
    for position in range(levels):
        result = result * 2 + ((value >> position) & 1)
    return result


def gather_rows(v, tail, n_px, n_py):
    height = v.shape[0]
    rows = height - tail
    line = np.arange(rows, dtype=np.int32)
    if (n_px, n_py) != (4, 8):
        groups = [list(range(0, n_py, 2)), list(range(1, n_py, 2))]
        got = lax.all_gather(lax.all_gather(v, "px", tiled=True), "py", axis_index_groups=groups, tiled=True)
        count = n_px * n_py // 2
        return [got], got.reshape(count, height, v.shape[1])[:, rows:], np.arange(count)[:, None] * height + line
    flip = lambda u, axis, n, m: lax.ppermute(u, axis, [(i, i ^ m) for i in range(n)])
    across = lambda u, m: flip(u, "py", n_py, m)
    half, rest = rows // 2, height - rows // 2
    blocks, tails, places = [], [], []

    def add(u):
        blocks.append(u)
        return sum(b.shape[0] for b in blocks[:-1])

    def add_whole(u):
        places.append(add(u) + line)
        tails.append(u[rows:])

    columns = [v] + [flip(v, "px", n_px, m) for m in range(1, n_px)]
    for members in ([0, 1], [2], [3]):
        one = [across(columns[m], 2) for m in members]
        two = [across(columns[m], 4) for m in members]
        upper = across(jnp.concatenate([u[:half] for u in one], 0), 4)
        lower = across(jnp.concatenate([u[half:] for u in two], 0), 2)
        for u in [columns[m] for m in members] + one + two:
            add_whole(u)
        at_upper, at_lower = add(upper), add(lower)
        for i in range(len(members)):
            places.append(np.concatenate([at_upper + i * half + line[:half], at_lower + i * rest + line[: rows - half]]))
            tails.append(lower[i * rest + rows - half : (i + 1) * rest])
    return blocks, jnp.stack(tails), np.stack(places)


def local(positions, strength, destination, tile_index, particle_count):
    rows, _, width = positions.shape
    n_px, n_py = lax.axis_size("px"), lax.axis_size("py")
    me_x, me_y = lax.axis_index("px"), lax.axis_index("py")
    width_x, width_y = NX // n_px, NY // n_py
    tiles_x, tiles_y = width_x // BX, width_y // BY
    tiles = tiles_x * tiles_y
    assert n_py >= 2 * n_px
    classes = n_py // 2
    res_x = reverse_digits(me_x, n_px.bit_length() - 1)
    res_y = reverse_digits(me_y, n_py.bit_length() - 1)
    side = me_y & 1
    low_y = res_y % classes

    alive = jnp.arange(width, dtype=jnp.int32)[None, :] < particle_count[:, None]
    live = jnp.where(alive, strength, jnp.zeros_like(strength))
    packed = jnp.concatenate([positions.reshape(rows, 3 * width), live], 1)
    info = (destination[:, 0] * tiles + tile_index).astype(jnp.float32)
    tail = -(-rows // (4 * width) // 8) * 8
    info = jnp.pad(info, (0, tail * 4 * width - rows)).reshape(tail, 4 * width)
    blocks, tails, places = gather_rows(jnp.concatenate([packed, info], 0), tail, n_px, n_py)
    info = tails.reshape(tails.shape[0], -1)[:, :rows].astype(jnp.int32)
    number = jnp.asarray(places, jnp.int32)
    radix = 2 * sum(b.shape[0] for b in blocks)

    pencil, tile = info // tiles, info % tiles
    at_x, at_y = pencil // n_py, pencil % n_py
    k = (res_x * at_x * (n_py // n_px) + low_y * at_y) % n_py
    half = k % classes
    group = tile * classes + (half - (half & 1)) + (at_y & 1)
    code = group * radix + number * 2 + (k >= classes).astype(jnp.int32)
    plan = make_plan(lax.sort(code.reshape(-1)), radix, tiles * classes, tiles_y * classes, STEP_ROWS)

    c = jnp.arange(classes, dtype=jnp.int32)
    odd = c & 1
    exponent = jnp.where(low_y % 2 == 1, c, c - odd).astype(jnp.float32) * (2.0 * math.pi / n_py)
    flip = (1 - 2 * (odd * side)).astype(jnp.float32)
    coef = jnp.concatenate([jnp.cos(exponent) * flip, -jnp.sin(exponent) * flip])

    matrix_y = dft_matrix(res_y, n_py, width_y, NY, 1.0 / math.sqrt(NX * NY))
    matrix_x = dft_matrix(res_x, n_px, width_x, NX, 1.0)
    swap = [(i, i ^ 1) for i in range(n_py)]
    last = max(1, tiles_x // 4)
    halves = []
    for first, each in ((0, tiles_x - last), (tiles_x - last, last)):
        own, other = deposit(plan, blocks, coef, first, each, tiles_y, classes, STEP_ROWS, DEPTH)
        halves.append((own, lax.ppermute(other, "py", swap)))
    return transform(matrix_y, matrix_x, halves)


def solution(mesh):
    placed = (
        P(("px", "py"), None, None),
        P(("px", "py"), None),
        P(("px", "py"), None),
        P(("px", "py")),
        P(("px", "py")),
    )
    return jax.shard_map(
        local, mesh=mesh, in_specs=placed, out_specs=P(None, "px", "py", None), check_vma=False
    )
```

```python
import functools
import math

import jax
import jax.numpy as jnp
import numpy as np
from jax import lax
from jax.experimental import pallas as pl
from jax.experimental.pallas import tpu as pltpu
from jax.sharding import PartitionSpec as P

NX = 512
NY = 512
NZ = 256
BX = 16
BY = 8
BF = jnp.bfloat16
VMEM = 56 << 20
STEP_ROWS = 2
PAIR = 2
DEPTH = 32
LANES = 128


def spline(offset):
    a = jnp.abs(offset)
    b = jnp.maximum(2.0 - a, 0.0)
    inner = (1.5 * a - 2.5) * (a * a) + 1.0
    outer = (b * b) * (0.5 * b - 0.5)
    return jnp.where(a < 1.0, inner, outer)


def split(v):
    hi = v.astype(BF)
    return hi, (v - hi.astype(jnp.float32)).astype(BF)


def dot(a, b):
    return jnp.dot(a, b, preferred_element_type=jnp.float32)


def fill(x, y, z, w):
    width = x.shape[1]
    ix = lax.broadcasted_iota(jnp.int32, (BX, width), 0).astype(jnp.float32)
    iy = lax.broadcasted_iota(jnp.int32, (BY, width), 0).astype(jnp.float32)
    wx = spline(x - ix)
    wy = spline(y - iy) * w
    planar_hi, planar_lo, depth_hi, depth_lo = [], [], [], []
    for i in range(0, BX, 2):
        hi, lo = split(jnp.concatenate([wx[i : i + 1] * wy, wx[i + 1 : i + 2] * wy], 0))
        planar_hi.append(hi)
        planar_lo.append(lo)
    q0 = jnp.floor((z - 1.0) * 0.0625)
    away = (z - 16.0 * q0) - ix
    far = away > 8.0
    hi, lo = split(spline(jnp.where(far, away - 16.0, away)))
    block = jnp.where(far, q0 + 1.0, q0).astype(BF)
    spread = lambda v: jnp.concatenate([v] * (LANES // 16), 0).T
    hi, lo, block = spread(hi), spread(lo), spread(block)
    zero = jnp.zeros((width, LANES), BF)
    column_block = (lax.broadcasted_iota(jnp.int32, (width, LANES), 1) // 16).astype(jnp.float32)
    for t in range(NZ // LANES):
        here = block == (column_block + float(t * (LANES // 16))).astype(BF)
        depth_hi.append(jnp.where(here, hi, zero))
        depth_lo.append(jnp.where(here, lo, zero))
    return [jnp.concatenate(v, 0) for v in (planar_hi, planar_lo)] + [jnp.concatenate(v, 1) for v in (depth_hi, depth_lo)]


def deposit_kernel(
    groups_of, firsts, ends, order, span, coef, *refs, classes, ch, depth, first, blocks
):
    parts, (own, other, acc, data, arrived) = refs[:blocks], refs[blocks:]
    tile = pl.program_id(0) * pl.num_programs(1) + pl.program_id(1)
    width = data.shape[1] // 4
    base = first * pl.num_programs(1) * classes

    def multiply(t, stop):
        live = t < stop
        t = jnp.minimum(t, groups_of.shape[0] - 1)
        j0, e = firsts[t], jnp.where(live, ends[t], 0)
        g = jnp.where(live, groups_of[t] - base, acc.shape[0] - 1)
        v = None
        for u in range(0, ch, PAIR):
            made = []
            for j in range(u, u + PAIR):
                entry = order[jnp.minimum(j0 + j, order.shape[0] - 1)]
                sign = jnp.where(j0 + j < e, (1 - 2 * (entry & 1)).astype(jnp.float32), 0.0)
                row = data[pl.ds(entry >> 1, 1), :]
                x, y, z, w = (row[:, k * width : (k + 1) * width] for k in range(4))
                made.append(fill(x, y, z, w * sign))
            ph, plo = (jnp.concatenate([m[k] for m in made], 1) for k in range(2))
            dh, dl = (jnp.concatenate([m[k] for m in made], 0) for k in range(2, 4))
            cells = ph.shape[0]
            both = dot(jnp.concatenate([ph, plo], 0), dh)
            p = both[:cells] + both[cells:] + dot(ph, dl)
            v = p if v is None else v + p
        acc[g] += v

    @pl.when(tile == 0)
    def _():
        copies, at = [], 0
        for k, part in enumerate(parts):
            rows = part.shape[0]
            copies.append(pltpu.make_async_copy(part, data.at[at : at + rows], arrived.at[k]))
            at += rows
        for copy in copies:
            copy.start()

        def clear(i, _):
            acc[i] = jnp.zeros(acc.shape[1:], jnp.float32)
            return 0

        lax.fori_loop(0, acc.shape[0], clear, 0)
        for copy in copies:
            copy.wait()
        begin, stop = span[first], span[first + pl.num_programs(0)]

        def step(i, _):
            for k in range(depth):
                t = begin + i * depth + k
                multiply(t, stop)
            return 0

        lax.fori_loop(0, (stop - begin + depth - 1) // depth, step, 0)

    for m in range(2):
        even, odd = (
            functools.reduce(
                jnp.add, [coef[m * classes + c] * acc[tile * classes + c] for c in range(parity, classes, 2)]
            )
            for parity in range(2)
        )
        own[m] = (even + odd).reshape(BX, BY, NZ)
        other[m] = (even - odd).reshape(BX, BY, NZ)


def deposit(plan, blocks, coef, first, tiles_x, tiles_y, classes, ch, depth):
    rows, lanes = sum(b.shape[0] for b in blocks), blocks[0].shape[1]
    width = lanes // 4
    spec = lambda: pl.BlockSpec((2, BX, BY, NZ), lambda i, j, *_: (0, i, j, 0))
    shape = jax.ShapeDtypeStruct((2, tiles_x * BX, tiles_y * BY, NZ), jnp.float32)
    flops = 6 * rows * BX * BY * NZ * width * tiles_x // 8
    return pl.pallas_call(
        functools.partial(deposit_kernel, classes=classes, ch=ch, depth=depth, first=first, blocks=len(blocks)),
        grid_spec=pltpu.PrefetchScalarGridSpec(
            num_scalar_prefetch=5,
            grid=(tiles_x, tiles_y),
            in_specs=[pl.BlockSpec(memory_space=pltpu.SMEM)] + [pl.BlockSpec(memory_space=pl.ANY)] * len(blocks),
            out_specs=[spec(), spec()],
            scratch_shapes=[
                pltpu.VMEM((tiles_x * tiles_y * classes + 1, BX * BY, NZ), jnp.float32),
                pltpu.VMEM((rows, lanes), jnp.float32),
                pltpu.SemaphoreType.DMA((len(blocks),)),
            ],
        ),
        out_shape=[shape, shape],
        compiler_params=pltpu.CompilerParams(vmem_limit_bytes=VMEM),
        cost_estimate=pl.CostEstimate(flops=flops, bytes_accessed=rows * lanes * 4, transcendentals=0),
    )(*plan, coef, *blocks)


def make_plan(code, radix, group_count, span_groups, ch):
    total = code.shape[0]
    edges = jnp.arange(group_count + 1, dtype=jnp.int32) * radix
    start = jnp.sum((code[None, :] < edges[:, None]).astype(jnp.int32), axis=1)
    steps = (start[1:] - start[:-1] + ch - 1) // ch
    before = jnp.sum(jnp.where(jnp.tri(group_count, k=-1, dtype=jnp.bool_), steps[None, :], 0), axis=1)
    after = before + steps
    t = jnp.arange(total // ch + group_count, dtype=jnp.int32)[:, None]
    mine = (before[None, :] <= t) & (t < after[None, :])
    pick = lambda v: jnp.sum(jnp.where(mine, v, 0), axis=1)
    group = pick(jnp.arange(group_count, dtype=jnp.int32)[None, :])
    first = pick(start[None, :-1] + (t - before[None, :]) * ch)
    end = pick(jnp.broadcast_to(start[None, 1:], mine.shape))
    span = jnp.concatenate([before[::span_groups], after[-1:]])
    return group, first, end, code % radix, span


def transform_kernel(yh, yl, xh, xl, *refs, counts):
    out, held = refs[-2:]
    t = pl.program_id(0)
    wide_y, wide_x = held.shape[2], held.shape[1]

    begin = 0
    for n, (own, got) in zip(counts, zip(refs[0:-2:2], refs[1:-2:2])):

        @pl.when((t >= begin) & (t < begin + n))
        def _(own=own, got=got):
            def one(i, _):
                u = jnp.concatenate([own[0, i] + got[0, i], own[1, i] + got[1, i]], 0)
                hi, lo = split(u)
                r = dot(yh[...], jnp.concatenate([hi, lo], 0)) + dot(yl[...], hi)
                held[0, t * BX + i] = r[:wide_y]
                held[1, t * BX + i] = r[wide_y:]
                return 0

            lax.fori_loop(0, BX, one, 0, unroll=8)

        begin += n

    @pl.when(t >= begin)
    def _():
        at = pl.multiple_of((t - begin) * 8, 8)
        u = jnp.concatenate([jnp.swapaxes(held[c, :, pl.ds(at, 8), :], 0, 1) for c in range(2)], 1)
        done = []
        for k in range(8):
            hi, lo = split(u[k])
            done.append(dot(xh[...], hi) + dot(xl[...], hi) + dot(xh[...], lo))
        w = jnp.stack(done)
        out[0] = jnp.swapaxes(w[:, :wide_x], 0, 1)
        out[1] = jnp.swapaxes(w[:, wide_x:], 0, 1)


def transform(matrix_y, matrix_x, halves):
    (yh, yl), (xh, xl) = matrix_y, matrix_x
    yh = jnp.concatenate([yh, yh], 1)
    _, _, y, z = halves[0][0].shape
    counts = [own.shape[1] // BX for own, _ in halves]
    whole = lambda m: pl.BlockSpec(m.shape, lambda t: (0, 0))
    specs, begin = [], 0
    for n in counts:
        spec = pl.BlockSpec((2, BX, y, z), lambda t, n=n, begin=begin: (0, jnp.clip(t - begin, 0, n - 1), 0, 0))
        specs += [spec, spec]
        begin += n
    x = begin * BX
    return pl.pallas_call(
        functools.partial(transform_kernel, counts=counts),
        grid=(begin + y // 8,),
        in_specs=[whole(yh), whole(yl), whole(xh), whole(xl)] + specs,
        out_specs=pl.BlockSpec((2, x, 8, z), lambda t: (0, 0, jnp.maximum(t - begin, 0), 0)),
        out_shape=jax.ShapeDtypeStruct((2, x, y, z), jnp.float32),
        scratch_shapes=[pltpu.VMEM((2, x, y, z), jnp.float32)],
        compiler_params=pltpu.CompilerParams(vmem_limit_bytes=VMEM),
    )(yh, yl, xh, xl, *[v for half in halves for v in half])


def dft_matrix(first, step, cells, total, scale):
    i = jnp.arange(cells, dtype=jnp.int32)
    angle = (2.0 * math.pi / total) * ((first + step * i)[:, None] * i[None, :] % total).astype(jnp.float32)
    c, s = jnp.cos(angle) * scale, jnp.sin(angle) * scale
    m = jnp.concatenate([jnp.concatenate([c, s], 1), jnp.concatenate([-s, c], 1)], 0)
    hi = lax.reduce_precision(m, 8, 7)
    return hi.astype(BF), (m - hi).astype(BF)


def reverse_digits(value, levels):
    result = 0
    for position in range(levels):
        result = result * 2 + ((value >> position) & 1)
    return result


def gather_rows(v, tail, n_px, n_py):
    height = v.shape[0]
    rows = height - tail
    line = np.arange(rows, dtype=np.int32)
    if (n_px, n_py) != (4, 8):
        groups = [list(range(0, n_py, 2)), list(range(1, n_py, 2))]
        got = lax.all_gather(lax.all_gather(v, "px", tiled=True), "py", axis_index_groups=groups, tiled=True)
        count = n_px * n_py // 2
        return [got], got.reshape(count, height, v.shape[1])[:, rows:], np.arange(count)[:, None] * height + line
    flip = lambda u, axis, n, m: lax.ppermute(u, axis, [(i, i ^ m) for i in range(n)])
    across = lambda u, m: flip(u, "py", n_py, m)
    half, rest = rows // 2, height - rows // 2
    blocks, tails, places = [], [], []

    def add(u):
        blocks.append(u)
        return sum(b.shape[0] for b in blocks[:-1])

    def add_whole(u):
        places.append(add(u) + line)
        tails.append(u[rows:])

    columns = [v] + [flip(v, "px", n_px, m) for m in range(1, n_px)]
    for members in ([0], [1], [2], [3]):
        one = [across(columns[m], 2) for m in members]
        two = [across(columns[m], 4) for m in members]
        upper = across(jnp.concatenate([u[:half] for u in one], 0), 4)
        lower = across(jnp.concatenate([u[half:] for u in two], 0), 2)
        for u in [columns[m] for m in members] + one + two:
            add_whole(u)
        at_upper, at_lower = add(upper), add(lower)
        for i in range(len(members)):
            places.append(np.concatenate([at_upper + i * half + line[:half], at_lower + i * rest + line[: rows - half]]))
            tails.append(lower[i * rest + rows - half : (i + 1) * rest])
    return blocks, jnp.stack(tails), np.stack(places)


def local(positions, strength, destination, tile_index, particle_count):
    rows, _, width = positions.shape
    n_px, n_py = lax.axis_size("px"), lax.axis_size("py")
    me_x, me_y = lax.axis_index("px"), lax.axis_index("py")
    width_x, width_y = NX // n_px, NY // n_py
    tiles_x, tiles_y = width_x // BX, width_y // BY
    tiles = tiles_x * tiles_y
    assert n_py >= 2 * n_px
    classes = n_py // 2
    res_x = reverse_digits(me_x, n_px.bit_length() - 1)
    res_y = reverse_digits(me_y, n_py.bit_length() - 1)
    side = me_y & 1
    low_y = res_y % classes

    alive = jnp.arange(width, dtype=jnp.int32)[None, :] < particle_count[:, None]
    live = jnp.where(alive, strength, jnp.zeros_like(strength))
    packed = jnp.concatenate([positions.reshape(rows, 3 * width), live], 1)
    info = (destination[:, 0] * tiles + tile_index).astype(jnp.float32)
    tail = -(-rows // (4 * width) // 8) * 8
    info = jnp.pad(info, (0, tail * 4 * width - rows)).reshape(tail, 4 * width)
    blocks, tails, places = gather_rows(jnp.concatenate([packed, info], 0), tail, n_px, n_py)
    info = tails.reshape(tails.shape[0], -1)[:, :rows].astype(jnp.int32)
    number = jnp.asarray(places, jnp.int32)
    radix = 2 * sum(b.shape[0] for b in blocks)

    pencil, tile = info // tiles, info % tiles
    at_x, at_y = pencil // n_py, pencil % n_py
    k = (res_x * at_x * (n_py // n_px) + low_y * at_y) % n_py
    half = k % classes
    group = tile * classes + (half - (half & 1)) + (at_y & 1)
    code = group * radix + number * 2 + (k >= classes).astype(jnp.int32)
    plan = make_plan(lax.sort(code.reshape(-1)), radix, tiles * classes, tiles_y * classes, STEP_ROWS)

    c = jnp.arange(classes, dtype=jnp.int32)
    odd = c & 1
    exponent = jnp.where(low_y % 2 == 1, c, c - odd).astype(jnp.float32) * (2.0 * math.pi / n_py)
    flip = (1 - 2 * (odd * side)).astype(jnp.float32)
    coef = jnp.concatenate([jnp.cos(exponent) * flip, -jnp.sin(exponent) * flip])

    matrix_y = dft_matrix(res_y, n_py, width_y, NY, 1.0 / math.sqrt(NX * NY))
    matrix_x = dft_matrix(res_x, n_px, width_x, NX, 1.0)
    swap = [(i, i ^ 1) for i in range(n_py)]
    last = max(1, tiles_x // 8)
    halves = []
    for first, each in ((0, tiles_x - last), (tiles_x - last, last)):
        own, other = deposit(plan, blocks, coef, first, each, tiles_y, classes, STEP_ROWS, DEPTH)
        halves.append((own, lax.ppermute(other, "py", swap)))
    return transform(matrix_y, matrix_x, halves)


def solution(mesh):
    placed = (
        P(("px", "py"), None, None),
        P(("px", "py"), None),
        P(("px", "py"), None),
        P(("px", "py")),
        P(("px", "py")),
    )
    return jax.shard_map(
        local, mesh=mesh, in_specs=placed, out_specs=P(None, "px", "py", None), check_vma=False
    )
```
